32 devices in a mesh: groups: 2 (over y), ao: 4 (over z), aux: 2 (over x), occ: 2 (over core).
Axes of the slice: x: 2, y: 2, z: 4, core: 2. Of those that a mesh axis runs over, the one named last changes fastest.
Arguments:
- slab: bfloat16 [40, 3072, 3072], P(('groups', 'aux'), 'ao'), parts along dimension 0, may hold values from -6 to 6
- coeffs: bfloat16 [6144, 384], P(('groups', 'ao')), parts along dimension 0, may hold values from -0.109375 to 0.109375
- atom_of: int32 [6144], P(('groups', 'ao')), parts along dimension 0, may hold values from 0 to 399, never falling along the last dimension, each value on 1 to 16 neighbouring positions
Outputs:
- gradient: float32 [6144, 384], P(('groups', 'ao'), ('aux', 'occ')), parts along dimension 0
- atom_energy: float32 [800], P('groups'), parts along dimension 0
The draws below stay inside these ranges and needn't reach their ends.
There are 2 independent parts, one for each index of `groups`. The reference program is written for one: setup_inputs(seed, part) draws one part's arguments, and reference() takes and returns one part's arrays. A program takes and returns all parts, laid end to end along the dimension named above; each array names one. Nothing has to cross between parts.
Inputs may be any that keep to these rules, and one draw needn't show every extreme that they name: atom_of never falls along the basis functions; each atom holds 1 to 16 functions, and some atom exactly 16.
All inputs are finite; a program needn't handle non-finite values.
Results may differ from the reference program's by a relative error of at most 0.0027.
Values may be sent and summed in bfloat16 or wider, within the bound.
A program may use at most 128 MiB of HBM per device.

```python
import math
import jax
import jax.numpy as jnp
import numpy as np
from jax import lax

NAO = 3072
NOCC = 384
NATOM = 400
SEG_MOST = 16
NAUX = 20


def level_of(key, shape, cuts, smallest, top_value):
    gain = 1.0
    for position, shards_of in cuts:
        heights = jax.random.uniform(jax.random.fold_in(jax.random.fold_in(key, 6), position), (shards_of,), jnp.float32, smallest / len(cuts), top_value / len(cuts))
        gain = gain * jnp.repeat(jnp.exp(heights), shape[position] // shards_of).reshape((-1,) + (1,) * (len(shape) - 1 - position))
    return gain


def profile(amount, total, limit, skew):
    portions = [(1 << 20) // math.isqrt(rank ** skew) + 1 for rank in range(2, amount + 1)]
    spare, holding = total - limit - (amount - 1), [1] * (amount - 1)
    while spare > 0:
        movable = [i for i in range(amount - 1) if holding[i] < limit]
        whole, remaining = sum([portions[i] for i in movable]), spare
        for i in movable:
            extra = min(limit - holding[i], max(1, remaining * portions[i] // whole), spare)
            holding[i] = holding[i] + extra
            spare = spare - extra
    return np.array([limit] + holding)


def uneven_parts(key, number_of, total, limit, slope):
    if number_of == 2:
        one = jax.random.randint(key, (), max(1, total - limit), min(limit, total - 1) + 1)
        return jnp.stack([one, total - one])
    tallies = jnp.asarray(profile(number_of, total, limit, slope), jnp.int32)
    twos = (number_of - 1) // 2
    donor, sink = tallies[1:1 + 2 * twos:2], tallies[2:2 + 2 * twos:2]
    room = jnp.minimum(donor - 1, limit - sink)
    shifted = jax.random.randint(jax.random.fold_in(key, 1), (twos,), 0, 1 << 20) % (room + 1)
    tallies = tallies.at[1:1 + 2 * twos:2].set(donor - shifted).at[2:2 + 2 * twos:2].set(sink + shifted)
    return tallies[jax.random.permutation(jax.random.fold_in(key, 2), number_of)]


def noise(rng, dims, width, bound, pieces=(), kind=jnp.bfloat16):
    factor_of = level_of(rng, dims, pieces, -0.22, 0.18) if pieces else 1.0
    entries = jax.random.normal(rng, dims, jnp.float32) * width * factor_of
    return jnp.minimum(jnp.maximum(entries, -bound), bound).astype(kind)


def setup_inputs(seed: int = 0, part: int = 0) -> dict:
    key_list = jax.random.split(jax.random.key(seed), 4)
    own_keys = jax.random.split(jax.random.fold_in(key_list[3], part), 4)
    slab = noise(own_keys[0], (NAUX, NAO, NAO), 1.0, 6.0, ((0, 2), (1, 4)))
    coeffs = noise(own_keys[1], (NAO, NOCC), NAO ** -0.5, 0.109375, ((0, 4),))
    atom_of = jnp.searchsorted(jnp.cumsum(uneven_parts(own_keys[2], NATOM, NAO, SEG_MOST, 2)), jnp.arange(NAO), side="right").astype(jnp.int32)
    return dict(slab=slab, coeffs=coeffs, atom_of=atom_of)


def reference(slab, coeffs, atom_of):

    def half_one(rows):
        return jnp.dot(rows, coeffs, preferred_element_type=jnp.float32).astype(jnp.bfloat16)
    half = lax.map(half_one, slab)
    coeff_wide = coeffs.astype(jnp.float32)
    half_wide = half.astype(jnp.float32)
    pairs = jnp.einsum('pmi,mj->pij', half_wide, coeff_wide).astype(jnp.bfloat16)
    normalizer = 1.0 / jnp.sqrt(jnp.float32(NAUX * NOCC))
    gradient = jnp.einsum('pmi,pij->mj', half_wide, pairs.astype(jnp.float32)) * normalizer
    weighted = lax.optimization_barrier(jnp.sum(coeff_wide * gradient, axis=1))
    onehot = (atom_of[:, None] == jnp.arange(NATOM, dtype=jnp.int32)[None, :]).astype(jnp.float32)
    atom_energy = jnp.dot(weighted, onehot, precision=lax.Precision.HIGHEST)
    return (gradient, atom_energy)
```

```python
import functools

import jax
import jax.numpy as jnp
from jax import lax
from jax.experimental import pallas as pl
from jax.experimental.pallas import tpu as pltpu
from jax.sharding import PartitionSpec as P

NATOM = 400
MESH = pl.DeviceIdType.MESH
LAG = 2
SPLIT = 4


def kernel(
    dims, slab, coeffs, atom_of, grad_out, energy_out,
    slab_v, coeff_all, coeff_t, half, part, r_in, r_out, l_in, l_out, total, grad,
    sib, xout, xin, onehot, e_all,
    slab_sem, c_send_r, c_send_l, c_send_s, c_recv, c_recv_s,
    r_send, r_recv, l_send, l_recv, s_send, s_recv, x_send, x_recv, e_send, e_recv,
):
    n, nx, naux = dims
    rows, occ = coeffs.shape
    group_size = n * nx * 2
    chunks = naux * SPLIT
    height = occ // SPLIT
    width = occ // (nx * 2)
    z = lax.axis_index("ao")
    x = lax.axis_index("aux")
    c = lax.axis_index("occ")
    me = (z * nx + x) * 2 + c
    f32, bf16 = jnp.float32, jnp.bfloat16

    def slab_copy(p):
        return pltpu.make_async_copy(slab.at[c * naux + p], slab_v.at[p], slab_sem.at[p])

    for p in range(naux):
        slab_copy(p).start()

    barrier = pltpu.get_barrier_semaphore()

    def others(visit):
        def step(idx, carry):
            @pl.when(idx != me)
            def _():
                visit(idx, {"ao": idx // (nx * 2), "aux": (idx // 2) % nx, "occ": idx % 2})
            return carry
        lax.fori_loop(0, group_size, step, 0)

    others(lambda idx, dev: pl.semaphore_signal(barrier, inc=1, device_id=dev, device_id_type=MESH))
    pl.semaphore_wait(barrier, group_size - 1)

    def block(b, core):
        return coeff_all.at[pl.ds(pl.multiple_of(b * rows + core * (rows // 2), rows // 2), rows // 2)]

    def c_copy(b, dev, send, recv):
        return pltpu.make_async_remote_copy(
            src_ref=block(b, c), dst_ref=block(b, c), send_sem=send.at[b], recv_sem=recv.at[b],
            device_id=dev, device_id_type=MESH)

    def c_right(b):
        return c_copy(b, {"ao": z + 1}, c_send_r, c_recv)

    def c_left(b):
        return c_copy(b, {"ao": z - 1}, c_send_l, c_recv)

    def c_sib(b):
        return c_copy(b, {"occ": 1 - c}, c_send_s, c_recv_s)

    coeff_all[pl.ds(pl.multiple_of(z * rows, rows), rows), :] = coeffs[...]

    @pl.when(z + 1 < n)
    def _():
        c_right(z).start()

    @pl.when(z > 0)
    def _():
        c_left(z).start()

    coeff_t[...] = coeffs[...].astype(f32).T.astype(bf16)
    atoms = lax.broadcasted_iota(jnp.int32, (NATOM, rows), 0)
    onehot[...] = (atoms == atom_of[...]).astype(f32)
    grad[...] = jnp.zeros_like(grad)

    @pl.when(z == 0)
    def _():
        r_in[...] = jnp.zeros_like(r_in)

    @pl.when(z == n - 1)
    def _():
        l_in[...] = jnp.zeros_like(l_in)

    def gather_step(d, carry):
        @pl.when(z - d >= 0)
        def _():
            c_left(z - d).wait_recv()

            @pl.when(z + 1 < n)
            def _():
                c_right(z - d).start()
            c_sib(z - d).start()

        @pl.when(z + d < n)
        def _():
            c_right(z + d).wait_recv()

            @pl.when(z > 0)
            def _():
                c_left(z + d).start()
            c_sib(z + d).start()
        return carry

    lax.fori_loop(1, n, gather_step, 0)

    def gather_wait(b, carry):
        @pl.when(b != z)
        def _():
            pltpu.make_async_remote_copy(
                src_ref=block(b, 1 - c), dst_ref=block(b, 1 - c), send_sem=c_send_s.at[b],
                recv_sem=c_recv_s.at[b], device_id={"occ": 1 - c}, device_id_type=MESH).wait_recv()
        return carry

    lax.fori_loop(0, n, gather_wait, 0)

    mu = rows // 2

    def half_unit(p, unit):
        span = pl.ds(unit * mu, mu)
        half[p, span, :] = jnp.dot(
            slab_v[p, span, :], coeff_all[...], preferred_element_type=f32).astype(bf16)

    def part_unit(p):
        value = jnp.dot(coeff_t[...], half[p], preferred_element_type=f32)
        for k in range(SPLIT):
            part[p * SPLIT + k] = value[k * height:(k + 1) * height]

    def grad_unit(p):
        for k in range(SPLIT):
            grad[k * height:(k + 1) * height, :] += lax.dot_general(
                total[p * SPLIT + k], half[p], (((1,), (1,)), ((), ())), preferred_element_type=f32)

    def r_copy(i):
        return pltpu.make_async_remote_copy(
            src_ref=r_out.at[i], dst_ref=r_in.at[i], send_sem=r_send.at[i], recv_sem=r_recv.at[i],
            device_id={"ao": z + 1}, device_id_type=MESH)

    def l_copy(i):
        return pltpu.make_async_remote_copy(
            src_ref=l_out.at[i], dst_ref=l_in.at[i], send_sem=l_send.at[i], recv_sem=l_recv.at[i],
            device_id={"ao": z - 1}, device_id_type=MESH)

    def comm_slot(s):
        i_r = s - LAG * z
        i_l = s - LAG * (n - 1 - z)
        i_t = s - LAG * jnp.maximum(z, n - 1 - z)

        @pl.when((i_r >= 0) & (i_r < chunks))
        def _():
            @pl.when(z > 0)
            def _():
                r_copy(i_r).wait_recv()

            @pl.when(z + 1 < n)
            def _():
                r_out[i_r] = (part[i_r] + r_in[i_r].astype(f32)).astype(bf16)
                r_copy(i_r).start()

        @pl.when((i_l >= 0) & (i_l < chunks))
        def _():
            @pl.when(z + 1 < n)
            def _():
                l_copy(i_l).wait_recv()

            @pl.when(z > 0)
            def _():
                l_out[i_l] = (part[i_l] + l_in[i_l].astype(f32)).astype(bf16)
                l_copy(i_l).start()

        @pl.when((i_t >= 0) & (i_t < chunks))
        def _():
            total[i_t] = (
                part[i_t] + r_in[i_t].astype(f32) + l_in[i_t].astype(f32)).astype(bf16)

    slab_copy(0).wait()
    half_unit(0, 0)
    half_unit(0, 1)
    part_unit(0)

    delay = -(-LAG * (n - 1) // SPLIT)

    def group(g, carry):
        for k in range(SPLIT):
            comm_slot(g * SPLIT + k)
            if k < 3:
                @pl.when(g + 1 < naux)
                def _():
                    if k == 0:
                        slab_copy(g + 1).wait()
                    if k < 2:
                        half_unit(g + 1, k)
                    else:
                        part_unit(g + 1)
            else:
                @pl.when(g >= delay)
                def _():
                    grad_unit(g - delay)
        return carry

    lax.fori_loop(0, naux + delay, group, 0)

    def rows_of(x_to, core):
        return pl.ds(pl.multiple_of((x_to * 2 + core) * width, width), width)

    def s_copy(x_to):
        return pltpu.make_async_remote_copy(
            src_ref=grad.at[rows_of(x_to, 1 - c)], dst_ref=sib.at[x_to], send_sem=s_send.at[x_to],
            recv_sem=s_recv.at[x_to], device_id={"occ": 1 - c}, device_id_type=MESH)

    def x_copy(d):
        return pltpu.make_async_remote_copy(
            src_ref=xout.at[d - 1], dst_ref=xin.at[d - 1], send_sem=x_send.at[d - 1],
            recv_sem=x_recv.at[d - 1], device_id={"aux": lax.rem(x + d, nx)}, device_id_type=MESH)

    for d in range(1, nx + 1):
        s_copy(lax.rem(x + d, nx)).start()
    for d in range(1, nx + 1):
        x_to = lax.rem(x + d, nx)
        s_copy(x_to).wait_recv()
        both = grad[rows_of(x_to, c), :] + sib[x_to]
        if d < nx:
            xout[d - 1] = both.astype(bf16)
            x_copy(d).start()
    for d in range(1, nx):
        x_copy(d).wait_recv()
        both = both + xin[d - 1].astype(f32)
    normalizer = 1.0 / jnp.sqrt(jnp.float32(naux * 2 * nx * occ))
    both = both * normalizer
    grad_out[...] = both

    weighted = jnp.sum(coeff_t[rows_of(x, c), :].astype(f32) * both, axis=0, keepdims=True)
    e_all[me] = lax.dot_general(
        jnp.broadcast_to(weighted, (8, rows)), onehot[...], (((1,), (1,)), ((), ())),
        precision=lax.Precision.HIGHEST, preferred_element_type=f32)

    def e_copy(slot, peer, dev):
        return pltpu.make_async_remote_copy(
            src_ref=e_all.at[slot], dst_ref=e_all.at[slot], send_sem=e_send.at[peer],
            recv_sem=e_recv.at[slot], device_id=dev, device_id_type=MESH)

    others(lambda idx, dev: e_copy(me, idx, dev).start())

    def sent(i, carry):
        @pl.when(z + 1 < n)
        def _():
            r_copy(i).wait_send()

        @pl.when(z > 0)
        def _():
            l_copy(i).wait_send()
        return carry

    lax.fori_loop(0, chunks, sent, 0)

    def c_sent(b, carry):
        @pl.when((b <= z) & (z + 1 < n))
        def _():
            c_right(b).wait_send()

        @pl.when((b >= z) & (z > 0))
        def _():
            c_left(b).wait_send()

        @pl.when(b != z)
        def _():
            c_sib(b).wait_send()
        return carry

    lax.fori_loop(0, n, c_sent, 0)
    for d in range(1, nx + 1):
        s_copy(lax.rem(x + d, nx)).wait_send()
    for d in range(1, nx):
        x_copy(d).wait_send()
    others(lambda idx, dev: e_copy(idx, idx, dev).wait_recv())
    others(lambda idx, dev: e_copy(me, idx, dev).wait_send())
    energy_out[...] = lax.fori_loop(
        1, group_size, lambda i, acc: acc + e_all[i], e_all[0])


def shards(n, nx, slab, coeffs, atom_of):
    naux = slab.shape[0] // 2
    rows, occ = coeffs.shape
    nu = slab.shape[2]
    chunks, height, width = naux * SPLIT, occ // SPLIT, occ // (nx * 2)
    group_size = n * nx * 2
    bf16, f32 = jnp.bfloat16, jnp.float32
    dma = lambda k: pltpu.SemaphoreType.DMA((k,))
    vmem = pl.BlockSpec(memory_space=pltpu.VMEM)
    chunk = pltpu.VMEM((chunks, height, occ), bf16)
    macs = naux * rows * occ * (nu + 2 * occ)
    grad_t, energy = pl.pallas_call(
        functools.partial(kernel, (n, nx, naux)),
        out_shape=(
            jax.ShapeDtypeStruct((width, rows), f32),
            jax.ShapeDtypeStruct((8, NATOM), f32),
        ),
        in_specs=[pl.BlockSpec(memory_space=pl.ANY), vmem, vmem],
        out_specs=(vmem, vmem),
        scratch_shapes=[
            pltpu.VMEM((naux, rows, nu), bf16),
            pltpu.VMEM((nu, occ), bf16),
            pltpu.VMEM((occ, rows), bf16),
            pltpu.VMEM((naux, rows, occ), bf16),
            pltpu.VMEM((chunks, height, occ), f32),
            chunk, chunk, chunk, chunk, chunk,
            pltpu.VMEM((occ, rows), f32),
            pltpu.VMEM((nx, width, rows), f32),
            pltpu.VMEM((nx - 1, width, rows), bf16),
            pltpu.VMEM((nx - 1, width, rows), bf16),
            pltpu.VMEM((NATOM, rows), f32),
            pltpu.VMEM((group_size, 8, NATOM), f32),
            dma(naux), dma(n), dma(n), dma(n), dma(n), dma(n),
            dma(chunks), dma(chunks), dma(chunks), dma(chunks),
            dma(nx), dma(nx), dma(nx - 1), dma(nx - 1), dma(group_size), dma(group_size),
        ],
        compiler_params=pltpu.CompilerParams(
            collective_id=0, has_side_effects=True, vmem_limit_bytes=56 * 1024 * 1024),
        cost_estimate=pl.CostEstimate(
            flops=2 * macs, bytes_accessed=naux * rows * nu * 2, transcendentals=0),
    )(slab, coeffs, atom_of.reshape(1, rows))
    return grad_t.T, energy[0]


def solution(mesh):
    in_specs = (P(("groups", "aux"), "ao", None), P(("groups", "ao"), None), P(("groups", "ao")))
    out_specs = (P(("groups", "ao"), ("aux", "occ")), P("groups"))
    body = functools.partial(shards, mesh.shape["ao"], mesh.shape["aux"])
    return jax.shard_map(body, mesh=mesh, in_specs=in_specs, out_specs=out_specs, check_vma=False)
```

```python
import functools

import jax
import jax.numpy as jnp
from jax import lax
from jax.experimental import pallas as pl
from jax.experimental.pallas import tpu as pltpu
from jax.sharding import PartitionSpec as P

NATOM = 400
MESH = pl.DeviceIdType.MESH
LAG = 2
SPLIT = 3


def kernel(
    dims, slab, coeffs, atom_of, grad_out, energy_out,
    slab_v, coeff_all, coeff_t, half, part, r_in, r_out, l_in, l_out, total, grad,
    sib, xout, xin, onehot, e_all, w_sum,
    slab_sem, c_send_r, c_send_l, c_recv, c_send_s, c_recv_s, c_send_x, c_recv_x,
    r_send, r_recv, l_send, l_recv, s_send, s_recv, x_send, x_recv, e_send, e_recv,
):
    n, nx, naux, share = dims
    rows, occ = coeffs.shape
    group_size = n * nx * 2
    chunks = naux * SPLIT
    height = occ // SPLIT
    width = occ // (nx * 2)
    third = width // SPLIT
    piece = rows // (2 * share)
    z = lax.axis_index("ao")
    x = lax.axis_index("aux")
    c = lax.axis_index("occ")
    me = (z * nx + x) * 2 + c
    f32, bf16 = jnp.float32, jnp.bfloat16

    def slab_copy(p):
        return pltpu.make_async_copy(slab.at[c * naux + p], slab_v.at[p], slab_sem.at[p])

    for p in range(naux):
        slab_copy(p).start()

    barrier = pltpu.get_barrier_semaphore()

    def others(visit):
        def step(idx, carry):
            @pl.when(idx != me)
            def _():
                visit(idx, {"ao": idx // (nx * 2), "aux": (idx // 2) % nx, "occ": idx % 2})
            return carry
        lax.fori_loop(0, group_size, step, 0)

    others(lambda idx, dev: pl.semaphore_signal(barrier, inc=1, device_id=dev, device_id_type=MESH))
    pl.semaphore_wait(barrier, group_size - 1)

    xi = x if share > 1 else 0

    def c_copy(b, xx, dev, send, recv):
        ref = coeff_all.at[pl.ds(pl.multiple_of(b * rows + (xx * 2 + c) * piece, piece), piece)]
        return pltpu.make_async_remote_copy(
            src_ref=ref, dst_ref=ref, send_sem=send, recv_sem=recv, device_id=dev, device_id_type=MESH)

    def c_right(b):
        return c_copy(b, xi, {"ao": z + 1}, c_send_r.at[b], c_recv.at[b])

    def c_left(b):
        return c_copy(b, xi, {"ao": z - 1}, c_send_l.at[b], c_recv.at[b])

    def c_sib(b, xx):
        return c_copy(b, xx, {"occ": 1 - c}, c_send_s.at[b, xx], c_recv_s.at[b, xx])

    def c_across(b, d):
        return c_copy(b, xi, {"aux": lax.rem(x + d, nx)}, c_send_x.at[b, d], c_recv_x.at[b, xi])

    coeff_all[pl.ds(pl.multiple_of(z * rows, rows), rows), :] = coeffs[...]

    @pl.when(z + 1 < n)
    def _():
        c_right(z).start()

    @pl.when(z > 0)
    def _():
        c_left(z).start()

    turned = coeffs[...].astype(f32).T
    for k in range(SPLIT):
        for q in range(2 * nx):
            first = q * width + k * third
            coeff_t[k * height + q * third:k * height + (q + 1) * third, :] = (
                turned[first:first + third].astype(bf16))
    atoms = lax.broadcasted_iota(jnp.int32, (NATOM, rows), 0)
    onehot[...] = (atoms == atom_of[...].reshape(1, rows)).astype(f32)
    grad[...] = jnp.zeros_like(grad)

    @pl.when(z == 0)
    def _():
        r_in[...] = jnp.zeros_like(r_in)

    @pl.when(z == n - 1)
    def _():
        l_in[...] = jnp.zeros_like(l_in)

    def gather_step(d, carry):
        @pl.when((z - d >= 0) & (d < n))
        def _():
            b = z - d
            c_left(b).wait_recv()

            @pl.when(z + 1 < n)
            def _():
                c_right(b).start()
            for dx in range(1, share):
                c_across(b, dx).start()
            c_sib(b, xi).start()

        @pl.when((z + d < n) & (d < n))
        def _():
            b = z + d
            c_right(b).wait_recv()

            @pl.when(z > 0)
            def _():
                c_left(b).start()
            for dx in range(1, share):
                c_across(b, dx).start()
            c_sib(b, xi).start()

        def pass_on(b):
            for dx in range(1, share):
                xx = lax.rem(x + dx, nx)
                ref = coeff_all.at[pl.ds(pl.multiple_of(b * rows + (xx * 2 + c) * piece, piece), piece)]
                pltpu.make_async_remote_copy(
                    src_ref=ref, dst_ref=ref, send_sem=c_send_x.at[b, dx], recv_sem=c_recv_x.at[b, xx],
                    device_id={"aux": xx}, device_id_type=MESH).wait_recv()
                c_sib(b, xx).start()

        @pl.when((d > 1) & (z - d + 1 >= 0))
        def _():
            pass_on(z - d + 1)

        @pl.when((d > 1) & (z + d - 1 < n))
        def _():
            pass_on(z + d - 1)
        return carry

    lax.fori_loop(1, n + 1, gather_step, 0)

    def gather_wait(b, carry):
        @pl.when(b != z)
        def _():
            for xx in range(share):
                ref = coeff_all.at[
                    pl.ds(pl.multiple_of(b * rows + (xx * 2 + 1 - c) * piece, piece), piece)]
                pltpu.make_async_remote_copy(
                    src_ref=ref, dst_ref=ref, send_sem=c_send_s.at[b, xx], recv_sem=c_recv_s.at[b, xx],
                    device_id={"occ": 1 - c}, device_id_type=MESH).wait_recv()
        return carry

    lax.fori_loop(0, n, gather_wait, 0)

    mu = rows // 2

    def half_unit(p, unit):
        span = pl.ds(unit * mu, mu)
        half[p, span, :] = jnp.dot(
            slab_v[p, span, :], coeff_all[...], preferred_element_type=f32).astype(bf16)

    def part_unit(p):
        value = jnp.dot(coeff_t[...], half[p], preferred_element_type=f32)
        for k in range(SPLIT - 1):
            part[p * (SPLIT - 1) + k] = value[k * height:(k + 1) * height]
        part[naux * (SPLIT - 1) + p] = value[(SPLIT - 1) * height:]

    def grad_unit(p, k, i):
        grad[k] += lax.dot_general(
            total[i], half[p], (((1,), (1,)), ((), ())), preferred_element_type=f32)

    def rows_of(x_to, core):
        return pl.ds(pl.multiple_of((x_to * 2 + core) * third, third), third)

    def s_copy(k, x_to):
        return pltpu.make_async_remote_copy(
            src_ref=grad.at[k, rows_of(x_to, 1 - c)], dst_ref=sib.at[k, x_to],
            send_sem=s_send.at[k, x_to], recv_sem=s_recv.at[k, x_to], device_id={"occ": 1 - c},
            device_id_type=MESH)

    def x_copy(k, d):
        return pltpu.make_async_remote_copy(
            src_ref=xout.at[k, d], dst_ref=xin.at[k, d], send_sem=x_send.at[k, d],
            recv_sem=x_recv.at[k, d], device_id={"aux": lax.rem(x + d, nx)}, device_id_type=MESH)

    normalizer = 1.0 / jnp.sqrt(jnp.float32(naux * 2 * nx * occ))

    def across_cores(ks):
        for d in range(1, nx + 1):
            for k in ks:
                s_copy(k, lax.rem(x + d, nx)).start()

    def across_aux(ks):
        for d in range(1, nx + 1):
            x_to = lax.rem(x + d, nx)
            for k in ks:
                s_copy(k, x_to).wait_recv()
                both = grad[k, rows_of(x_to, c), :] + sib[k, x_to]
                if d < nx:
                    xout[k, d] = both.astype(bf16)
                    x_copy(k, d).start()
                else:
                    grad_out[k * third:(k + 1) * third, :] = both

    def finish(ks):
        for k in ks:
            span = slice(k * third, (k + 1) * third)
            both = grad_out[span, :]
            for d in range(1, nx):
                x_copy(k, d).wait_recv()
                both = both + xin[k, d].astype(f32)
            grad_out[span, :] = both * normalizer

    def weigh(k):
        value = coeff_t[k * height:(k + 1) * height, :].astype(f32) * grad[k]
        return jnp.sum(value, axis=0, keepdims=True)

    def r_copy(i):
        return pltpu.make_async_remote_copy(
            src_ref=r_out.at[i], dst_ref=r_in.at[i], send_sem=r_send.at[i], recv_sem=r_recv.at[i],
            device_id={"ao": z + 1}, device_id_type=MESH)

    def l_copy(i):
        return pltpu.make_async_remote_copy(
            src_ref=l_out.at[i], dst_ref=l_in.at[i], send_sem=l_send.at[i], recv_sem=l_recv.at[i],
            device_id={"ao": z - 1}, device_id_type=MESH)

    def comm_slot(s):
        i_r = s - LAG * z
        i_l = s - LAG * (n - 1 - z)
        i_t = s - LAG * jnp.maximum(z, n - 1 - z)

        @pl.when((i_r >= 0) & (i_r < chunks))
        def _():
            @pl.when(z > 0)
            def _():
                r_copy(i_r).wait_recv()

            @pl.when(z + 1 < n)
            def _():
                r_out[i_r] = (part[i_r] + r_in[i_r].astype(f32)).astype(bf16)
                r_copy(i_r).start()

        @pl.when((i_l >= 0) & (i_l < chunks))
        def _():
            @pl.when(z + 1 < n)
            def _():
                l_copy(i_l).wait_recv()

            @pl.when(z > 0)
            def _():
                l_out[i_l] = (part[i_l] + l_in[i_l].astype(f32)).astype(bf16)
                l_copy(i_l).start()

        @pl.when((i_t >= 0) & (i_t < chunks))
        def _():
            total[i_t] = (
                part[i_t] + r_in[i_t].astype(f32) + l_in[i_t].astype(f32)).astype(bf16)

    slab_copy(0).wait()
    half_unit(0, 0)
    half_unit(0, 1)
    part_unit(0)

    early = SPLIT - 1
    reach = LAG * (n - 1)
    done = early * (naux - 1) + reach + early - 1

    def slot(s, carry):
        comm_slot(s)
        p = s // early + 1
        for k in range(early):
            @pl.when((p < naux) & (lax.rem(s, early) == k))
            def _():
                if k == 0:
                    slab_copy(p).wait()
                    half_unit(p, 0)
                if k == 1:
                    half_unit(p, 1)
                if k == early - 1:
                    part_unit(p)
        t = s - reach - early + 1

        @pl.when((t >= 0) & (t <= early * (naux - 1)) & (lax.rem(t + early * n, early) == 0))
        def _():
            for k in range(early):
                grad_unit(t // early, k, t + k)

        @pl.when(s > done)
        def _():
            grad_unit(s - done - 1, early, early * naux + s - done - 1)

        @pl.when(s == done)
        def _():
            across_cores(range(early))

        @pl.when(s == done + 1)
        def _():
            w_sum[...] = sum(weigh(k) for k in range(early))

        @pl.when(s == done + 2)
        def _():
            across_aux(range(early))

        @pl.when(s == done + 4)
        def _():
            finish(range(early))
        return carry

    lax.fori_loop(0, chunks + reach, slot, 0)
    across_cores([early])

    weighted = (w_sum[...] + weigh(early)) * normalizer
    e_all[me] = lax.dot_general(
        jnp.broadcast_to(weighted, (8, rows)), onehot[...], (((1,), (1,)), ((), ())),
        precision=lax.Precision.HIGHEST, preferred_element_type=f32)

    def e_copy(slot, peer, dev):
        return pltpu.make_async_remote_copy(
            src_ref=e_all.at[slot], dst_ref=e_all.at[slot], send_sem=e_send.at[peer],
            recv_sem=e_recv.at[slot], device_id=dev, device_id_type=MESH)

    others(lambda idx, dev: e_copy(me, idx, dev).start())

    across_aux([early])
    finish([early])

    def sent(i, carry):
        @pl.when(z + 1 < n)
        def _():
            r_copy(i).wait_send()

        @pl.when(z > 0)
        def _():
            l_copy(i).wait_send()
        return carry

    lax.fori_loop(0, chunks, sent, 0)

    def c_sent(b, carry):
        @pl.when((b <= z) & (z + 1 < n))
        def _():
            c_right(b).wait_send()

        @pl.when((b >= z) & (z > 0))
        def _():
            c_left(b).wait_send()

        @pl.when(b != z)
        def _():
            for xx in range(share):
                c_sib(b, xx).wait_send()
            for dx in range(1, share):
                c_across(b, dx).wait_send()
        return carry

    lax.fori_loop(0, n, c_sent, 0)
    for k in range(SPLIT):
        for d in range(1, nx + 1):
            s_copy(k, lax.rem(x + d, nx)).wait_send()
        for d in range(1, nx):
            x_copy(k, d).wait_send()
    others(lambda idx, dev: e_copy(idx, idx, dev).wait_recv())
    others(lambda idx, dev: e_copy(me, idx, dev).wait_send())
    energy_out[...] = lax.fori_loop(
        1, group_size, lambda i, acc: acc + e_all[i], e_all[0])[0]


def shards(n, nx, slab, coeffs, atom_of):
    naux = slab.shape[0] // 2
    rows, occ = coeffs.shape
    nu = slab.shape[2]
    chunks, height, width = naux * SPLIT, occ // SPLIT, occ // (nx * 2)
    group_size = n * nx * 2
    bf16, f32 = jnp.bfloat16, jnp.float32
    third = width // SPLIT
    share = nx if rows % (32 * nx) == 0 else 1
    dma = lambda *k: pltpu.SemaphoreType.DMA(k)
    vmem = pl.BlockSpec(memory_space=pltpu.VMEM)
    chunk = pltpu.VMEM((chunks, height, occ), bf16)
    macs = naux * rows * occ * (nu + 2 * occ)
    grad_t, energy = pl.pallas_call(
        functools.partial(kernel, (n, nx, naux, share)),
        out_shape=(
            jax.ShapeDtypeStruct((width, rows), f32),
            jax.ShapeDtypeStruct((NATOM,), f32),
        ),
        in_specs=[pl.BlockSpec(memory_space=pl.ANY), vmem, vmem],
        out_specs=(vmem, vmem),
        scratch_shapes=[
            pltpu.VMEM((naux, rows, nu), bf16),
            pltpu.VMEM((nu, occ), bf16),
            pltpu.VMEM((occ, rows), bf16),
            pltpu.VMEM((naux, rows, occ), bf16),
            pltpu.VMEM((chunks, height, occ), f32),
            chunk, chunk, chunk, chunk, chunk,
            pltpu.VMEM((SPLIT, height, rows), f32),
            pltpu.VMEM((SPLIT, nx, third, rows), f32),
            pltpu.VMEM((SPLIT, nx, third, rows), bf16),
            pltpu.VMEM((SPLIT, nx, third, rows), bf16),
            pltpu.VMEM((NATOM, rows), f32),
            pltpu.VMEM((group_size, 8, NATOM), f32),
            pltpu.VMEM((1, rows), f32),
            dma(naux), dma(n), dma(n), dma(n),
            dma(n, share), dma(n, share), dma(n, share), dma(n, share),
            dma(chunks), dma(chunks), dma(chunks), dma(chunks),
            dma(SPLIT, nx), dma(SPLIT, nx), dma(SPLIT, nx), dma(SPLIT, nx), dma(group_size), dma(group_size),
        ],
        compiler_params=pltpu.CompilerParams(
            collective_id=0, has_side_effects=True, vmem_limit_bytes=56 * 1024 * 1024),
        cost_estimate=pl.CostEstimate(
            flops=2 * macs, bytes_accessed=naux * rows * nu * 2, transcendentals=0),
    )(slab, coeffs, atom_of)
    return grad_t.T, energy


def solution(mesh):
    in_specs = (P(("groups", "aux"), "ao", None), P(("groups", "ao"), None), P(("groups", "ao")))
    out_specs = (P(("groups", "ao"), ("aux", "occ")), P("groups"))
    body = functools.partial(shards, mesh.shape["ao"], mesh.shape["aux"])
    return jax.shard_map(body, mesh=mesh, in_specs=in_specs, out_specs=out_specs, check_vma=False)
```

```python
import functools

import jax
import jax.numpy as jnp
from jax import lax
from jax.experimental import pallas as pl
from jax.experimental.pallas import tpu as pltpu
from jax.sharding import PartitionSpec as P

NATOM = 400
MESH = pl.DeviceIdType.MESH
LAG = 2
SPLIT = 3

PIECES = 1


def kernel(
    dims, slab, coeffs, atom_of, grad_out, energy_out,
    slab_v, coeff_all, coeff_t, half, part, r_in, r_out, l_in, l_out, total, grad,
    sib, xout, xin, onehot, e_s, e_x, e_z, w_sum, acc,
    slab_sem, c_send_r, c_send_l, c_recv, c_send_s, c_recv_s, c_send_x, c_recv_x,
    r_send, r_recv, l_send, l_recv, s_send, s_recv, x_send, x_recv, es_send, es_recv, ex_send, ex_recv, ez_send, ez_recv,
):
    n, nx, naux, share = dims
    rows, occ = coeffs.shape
    chunks = naux * SPLIT
    height = occ // SPLIT
    width = occ // (nx * 2)
    third = width // SPLIT
    piece = rows // (2 * share)
    z = lax.axis_index("ao")
    x = lax.axis_index("aux")
    c = lax.axis_index("occ")
    f32, bf16 = jnp.float32, jnp.bfloat16

    def slab_copy(p):
        return pltpu.make_async_copy(slab.at[c * naux + p], slab_v.at[p], slab_sem.at[p])

    for p in range(naux):
        slab_copy(p).start()

    barrier = pltpu.get_barrier_semaphore()

    def along_ao(visit):
        def step(idx, carry):
            @pl.when(idx != z)
            def _():
                visit(idx, {"ao": idx})
            return carry
        lax.fori_loop(0, n, step, 0)

    def greet(dev):
        pl.semaphore_signal(barrier, inc=1, device_id=dev, device_id_type=MESH)

    along_ao(lambda idx, dev: greet(dev))
    greet({"occ": 1 - c})
    for d in range(1, nx):
        greet({"aux": lax.rem(x + d, nx)})
    pl.semaphore_wait(barrier, n - 1 + nx)

    xi = x if share > 1 else 0

    def c_copy(b, xx, dev, send, recv):
        ref = coeff_all.at[pl.ds(pl.multiple_of(b * rows + (xx * 2 + c) * piece, piece), piece)]
        return pltpu.make_async_remote_copy(
            src_ref=ref, dst_ref=ref, send_sem=send, recv_sem=recv, device_id=dev, device_id_type=MESH)

    def c_right(b):
        return c_copy(b, xi, {"ao": z + 1}, c_send_r.at[b], c_recv.at[b])

    def c_left(b):
        return c_copy(b, xi, {"ao": z - 1}, c_send_l.at[b], c_recv.at[b])

    def c_sib(b, xx):
        return c_copy(b, xx, {"occ": 1 - c}, c_send_s.at[b, xx], c_recv_s.at[b, xx])

    def c_across(b, d):
        return c_copy(b, xi, {"aux": lax.rem(x + d, nx)}, c_send_x.at[b, d], c_recv_x.at[b, xi])

    coeff_all[pl.ds(pl.multiple_of(z * rows, rows), rows), :] = coeffs[...]

    @pl.when(z + 1 < n)
    def _():
        c_right(z).start()

    @pl.when(z > 0)
    def _():
        c_left(z).start()

    turned = coeffs[...].astype(f32).T
    for k in range(SPLIT):
        for q in range(2 * nx):
            first = q * width + k * third
            coeff_t[k * height + q * third:k * height + (q + 1) * third, :] = (
                turned[first:first + third].astype(bf16))
    atoms = lax.broadcasted_iota(jnp.int32, (NATOM, rows), 0)
    onehot[...] = (atoms == atom_of[...].reshape(1, rows)).astype(f32)
    grad[...] = jnp.zeros_like(grad)

    @pl.when(z == 0)
    def _():
        r_in[...] = jnp.zeros_like(r_in)

    @pl.when(z == n - 1)
    def _():
        l_in[...] = jnp.zeros_like(l_in)

    def gather_step(d, carry):
        @pl.when((z - d >= 0) & (d < n))
        def _():
            b = z - d
            c_left(b).wait_recv()

            @pl.when(z + 1 < n)
            def _():
                c_right(b).start()
            for dx in range(1, share):
                c_across(b, dx).start()
            c_sib(b, xi).start()

        @pl.when((z + d < n) & (d < n))
        def _():
            b = z + d
            c_right(b).wait_recv()

            @pl.when(z > 0)
            def _():
                c_left(b).start()
            for dx in range(1, share):
                c_across(b, dx).start()
            c_sib(b, xi).start()

        def pass_on(b):
            for dx in range(1, share):
                xx = lax.rem(x + dx, nx)
                ref = coeff_all.at[pl.ds(pl.multiple_of(b * rows + (xx * 2 + c) * piece, piece), piece)]
                pltpu.make_async_remote_copy(
                    src_ref=ref, dst_ref=ref, send_sem=c_send_x.at[b, dx], recv_sem=c_recv_x.at[b, xx],
                    device_id={"aux": xx}, device_id_type=MESH).wait_recv()
                c_sib(b, xx).start()

        @pl.when((d > 1) & (z - d + 1 >= 0))
        def _():
            pass_on(z - d + 1)

        @pl.when((d > 1) & (z + d - 1 < n))
        def _():
            pass_on(z + d - 1)
        return carry

    def arrived(b):
        for xx in range(share):
            ref = coeff_all.at[
                pl.ds(pl.multiple_of(b * rows + (xx * 2 + 1 - c) * piece, piece), piece)]
            pltpu.make_async_remote_copy(
                src_ref=ref, dst_ref=ref, send_sem=c_send_s.at[b, xx], recv_sem=c_recv_s.at[b, xx],
                device_id={"occ": 1 - c}, device_id_type=MESH).wait_recv()

    by_block = rows % 128 == 0

    def consume(b):
        if by_block:
            span = pl.ds(pl.multiple_of(b * rows, rows), rows)
            acc[...] += jnp.dot(
                slab_v[0, :, span], coeff_all[span, :], preferred_element_type=f32)

    slab_copy(0).wait()
    acc[...] = jnp.zeros_like(acc)
    consume(z)

    def gather_and_use(d, carry):
        gather_step(d, carry)
        for b, there in ((z - d + 1, z - d + 1 >= 0), (z + d - 1, z + d - 1 < n)):
            @pl.when((d > 1) & there)
            def _():
                arrived(b)
                consume(b)
        return carry

    lax.fori_loop(1, n + 1, gather_and_use, 0)

    mu = rows // 2

    def half_unit(p, unit):
        span = pl.ds(unit * mu, mu)
        half[p, span, :] = jnp.dot(
            slab_v[p, span, :], coeff_all[...], preferred_element_type=f32).astype(bf16)

    def part_unit(p):
        value = jnp.dot(coeff_t[...], half[p], preferred_element_type=f32)
        for k in range(SPLIT - 1):
            part[p * (SPLIT - 1) + k] = value[k * height:(k + 1) * height]
        part[naux * (SPLIT - 1) + p] = value[(SPLIT - 1) * height:]

    def grad_unit(p, k, i):
        grad[k] += lax.dot_general(
            total[i], half[p], (((1,), (1,)), ((), ())), preferred_element_type=f32)

    def rows_of(x_to, core):
        return pl.ds(pl.multiple_of((x_to * 2 + core) * third, third), third)

    def s_copy(k, x_to):
        return pltpu.make_async_remote_copy(
            src_ref=grad.at[k, rows_of(x_to, 1 - c)], dst_ref=sib.at[k, x_to],
            send_sem=s_send.at[k, x_to], recv_sem=s_recv.at[k, x_to], device_id={"occ": 1 - c},
            device_id_type=MESH)

    def x_copy(k, d):
        return pltpu.make_async_remote_copy(
            src_ref=xout.at[k, d], dst_ref=xin.at[k, d], send_sem=x_send.at[k, d],
            recv_sem=x_recv.at[k, d], device_id={"aux": lax.rem(x + d, nx)}, device_id_type=MESH)

    normalizer = 1.0 / jnp.sqrt(jnp.float32(naux * 2 * nx * occ))

    def across_cores(ks):
        for d in range(1, nx + 1):
            for k in ks:
                s_copy(k, lax.rem(x + d, nx)).start()

    def across_aux(ks):
        for d in range(1, nx + 1):
            x_to = lax.rem(x + d, nx)
            for k in ks:
                s_copy(k, x_to).wait_recv()
                both = grad[k, rows_of(x_to, c), :] + sib[k, x_to]
                if d < nx:
                    xout[k, d] = both.astype(bf16)
                    x_copy(k, d).start()
                else:
                    grad_out[k * third:(k + 1) * third, :] = both

    def finish(ks):
        for k in ks:
            span = slice(k * third, (k + 1) * third)
            both = grad_out[span, :]
            for d in range(1, nx):
                x_copy(k, d).wait_recv()
                both = both + xin[k, d].astype(f32)
            grad_out[span, :] = both * normalizer

    def weigh(k):
        value = coeff_t[k * height:(k + 1) * height, :].astype(f32) * grad[k]
        return jnp.sum(value, axis=0, keepdims=True)

    low = height // PIECES

    def r_copy(i, h):
        return pltpu.make_async_remote_copy(
            src_ref=r_out.at[i, pl.ds(h * low, low)], dst_ref=r_in.at[i, pl.ds(h * low, low)],
            send_sem=r_send.at[i, h], recv_sem=r_recv.at[i, h],
            device_id={"ao": z + 1}, device_id_type=MESH)

    def l_copy(i, h):
        return pltpu.make_async_remote_copy(
            src_ref=l_out.at[i, pl.ds(h * low, low)], dst_ref=l_in.at[i, pl.ds(h * low, low)],
            send_sem=l_send.at[i, h], recv_sem=l_recv.at[i, h],
            device_id={"ao": z - 1}, device_id_type=MESH)

    def comm_slot(s):
        i_r = s - LAG * z
        i_l = s - LAG * (n - 1 - z)
        i_t = s - LAG * jnp.maximum(z, n - 1 - z)
        for h in range(PIECES):
            span = pl.ds(h * low, low)

            @pl.when((i_r >= 0) & (i_r < chunks))
            def _():
                @pl.when(z > 0)
                def _():
                    r_copy(i_r, h).wait_recv()

                @pl.when(z + 1 < n)
                def _():
                    r_out[i_r, span] = (part[i_r, span] + r_in[i_r, span].astype(f32)).astype(bf16)
                    r_copy(i_r, h).start()

            @pl.when((i_l >= 0) & (i_l < chunks))
            def _():
                @pl.when(z + 1 < n)
                def _():
                    l_copy(i_l, h).wait_recv()

                @pl.when(z > 0)
                def _():
                    l_out[i_l, span] = (part[i_l, span] + l_in[i_l, span].astype(f32)).astype(bf16)
                    l_copy(i_l, h).start()

        @pl.when((i_t >= 0) & (i_t < chunks))
        def _():
            total[i_t] = (
                part[i_t] + r_in[i_t].astype(f32) + l_in[i_t].astype(f32)).astype(bf16)

    if by_block:
        half[0] = acc[...].astype(bf16)
    else:
        half_unit(0, 0)
        half_unit(0, 1)
    part_unit(0)

    early = SPLIT - 1
    reach = LAG * (n - 1)
    done = early * (naux - 1) + reach + early - 1

    def slot(s, carry):
        comm_slot(s)
        p = s // early + 1
        for k in range(early):
            @pl.when((p < naux) & (lax.rem(s, early) == k))
            def _():
                if k == 0:
                    slab_copy(p).wait()
                    half_unit(p, 0)
                if k == 1:
                    half_unit(p, 1)
                if k == early - 1:
                    part_unit(p)
        t = s - reach - early + 1

        @pl.when((t >= 0) & (t <= early * (naux - 1)) & (lax.rem(t + early * n, early) == 0))
        def _():
            for k in range(early):
                grad_unit(t // early, k, t + k)

        @pl.when(s > done)
        def _():
            grad_unit(s - done - 1, early, early * naux + s - done - 1)

        @pl.when(s == done)
        def _():
            across_cores(range(early))

        @pl.when(s == done + 1)
        def _():
            w_sum[...] = sum(weigh(k) for k in range(early))

        @pl.when(s == done + 2)
        def _():
            across_aux(range(early))

        @pl.when(s == done + 4)
        def _():
            finish(range(early))
        return carry

    lax.fori_loop(0, chunks + reach, slot, 0)
    across_cores([early])

    weighted = (w_sum[...] + weigh(early)) * normalizer
    e_s[c] = lax.dot_general(
        jnp.broadcast_to(weighted, (8, rows)), onehot[...], (((1,), (1,)), ((), ())),
        precision=lax.Precision.HIGHEST, preferred_element_type=f32)

    def es_copy(core):
        return pltpu.make_async_remote_copy(
            src_ref=e_s.at[core], dst_ref=e_s.at[core], send_sem=es_send.at[0],
            recv_sem=es_recv.at[0], device_id={"occ": 1 - c}, device_id_type=MESH)

    def ex_copy(xx, d):
        return pltpu.make_async_remote_copy(
            src_ref=e_x.at[xx], dst_ref=e_x.at[xx], send_sem=ex_send.at[d],
            recv_sem=ex_recv.at[xx], device_id={"aux": lax.rem(x + d, nx)}, device_id_type=MESH)

    def ez_copy(slot, peer):
        return pltpu.make_async_remote_copy(
            src_ref=e_z.at[slot], dst_ref=e_z.at[slot], send_sem=ez_send.at[peer],
            recv_sem=ez_recv.at[slot], device_id={"ao": peer}, device_id_type=MESH)

    es_copy(c).start()
    across_aux([early])
    es_copy(1 - c).wait_recv()
    e_x[x] = e_s[0] + e_s[1]
    for d in range(1, nx):
        ex_copy(x, d).start()
    for d in range(1, nx):
        ex_copy(lax.rem(x + d, nx), d).wait_recv()
    e_z[z] = sum(e_x[k] for k in range(nx))
    along_ao(lambda idx, dev: ez_copy(z, idx).start())
    finish([early])

    def sent(i, carry):
        @pl.when(z + 1 < n)
        def _():
            for h in range(PIECES):
                r_copy(i, h).wait_send()

        @pl.when(z > 0)
        def _():
            for h in range(PIECES):
                l_copy(i, h).wait_send()
        return carry

    lax.fori_loop(0, chunks, sent, 0)

    def c_sent(b, carry):
        @pl.when((b <= z) & (z + 1 < n))
        def _():
            c_right(b).wait_send()

        @pl.when((b >= z) & (z > 0))
        def _():
            c_left(b).wait_send()

        @pl.when(b != z)
        def _():
            for xx in range(share):
                c_sib(b, xx).wait_send()
            for dx in range(1, share):
                c_across(b, dx).wait_send()
        return carry

    lax.fori_loop(0, n, c_sent, 0)
    for k in range(SPLIT):
        for d in range(1, nx + 1):
            s_copy(k, lax.rem(x + d, nx)).wait_send()
        for d in range(1, nx):
            x_copy(k, d).wait_send()
    es_copy(c).wait_send()
    for d in range(1, nx):
        ex_copy(x, d).wait_send()
    along_ao(lambda idx, dev: ez_copy(idx, idx).wait_recv())
    along_ao(lambda idx, dev: ez_copy(z, idx).wait_send())
    energy_out[...] = lax.fori_loop(1, n, lambda i, value: value + e_z[i], e_z[0])[0]


def shards(n, nx, slab, coeffs, atom_of):
    naux = slab.shape[0] // 2
    rows, occ = coeffs.shape
    nu = slab.shape[2]
    chunks, height, width = naux * SPLIT, occ // SPLIT, occ // (nx * 2)
    bf16, f32 = jnp.bfloat16, jnp.float32
    third = width // SPLIT
    share = nx if rows % (32 * nx) == 0 else 1
    dma = lambda *k: pltpu.SemaphoreType.DMA(k)
    vmem = pl.BlockSpec(memory_space=pltpu.VMEM)
    chunk = pltpu.VMEM((chunks, height, occ), bf16)
    macs = naux * rows * occ * (nu + 2 * occ)
    grad_t, energy = pl.pallas_call(
        functools.partial(kernel, (n, nx, naux, share)),
        out_shape=(
            jax.ShapeDtypeStruct((width, rows), f32),
            jax.ShapeDtypeStruct((NATOM,), f32),
        ),
        in_specs=[pl.BlockSpec(memory_space=pl.ANY), vmem, vmem],
        out_specs=(vmem, vmem),
        scratch_shapes=[
            pltpu.VMEM((naux, rows, nu), bf16),
            pltpu.VMEM((nu, occ), bf16),
            pltpu.VMEM((occ, rows), bf16),
            pltpu.VMEM((naux, rows, occ), bf16),
            pltpu.VMEM((chunks, height, occ), f32),
            chunk, chunk, chunk, chunk, chunk,
            pltpu.VMEM((SPLIT, height, rows), f32),
            pltpu.VMEM((SPLIT, nx, third, rows), f32),
            pltpu.VMEM((SPLIT, nx, third, rows), bf16),
            pltpu.VMEM((SPLIT, nx, third, rows), bf16),
            pltpu.VMEM((NATOM, rows), f32),
            pltpu.VMEM((2, 8, NATOM), f32),
            pltpu.VMEM((nx, 8, NATOM), f32),
            pltpu.VMEM((n, 8, NATOM), f32),
            pltpu.VMEM((1, rows), f32),
            pltpu.VMEM((rows, occ), f32),
            dma(naux), dma(n), dma(n), dma(n),
            dma(n, share), dma(n, share), dma(n, share), dma(n, share),
            dma(chunks, PIECES), dma(chunks, PIECES), dma(chunks, PIECES), dma(chunks, PIECES),
            dma(SPLIT, nx), dma(SPLIT, nx), dma(SPLIT, nx), dma(SPLIT, nx), dma(1), dma(1), dma(nx), dma(nx), dma(n), dma(n),
        ],
        compiler_params=pltpu.CompilerParams(
            collective_id=0, has_side_effects=True, vmem_limit_bytes=56 * 1024 * 1024),
        cost_estimate=pl.CostEstimate(
            flops=2 * macs, bytes_accessed=naux * rows * nu * 2, transcendentals=0),
    )(slab, coeffs, atom_of)
    return grad_t.T, energy


def solution(mesh):
    in_specs = (P(("groups", "aux"), "ao", None), P(("groups", "ao"), None), P(("groups", "ao")))
    out_specs = (P(("groups", "ao"), ("aux", "occ")), P("groups"))
    body = functools.partial(shards, mesh.shape["ao"], mesh.shape["aux"])
    return jax.shard_map(body, mesh=mesh, in_specs=in_specs, out_specs=out_specs, check_vma=False)
```
